512 devices in a mesh: tm: 128 (over z_lo, x, y, core), rows: 4 (over z_hi).
Axes of the slice: x: 4, y: 8, z: 8 (z_hi: 4, z_lo: 2; z = z_hi * 2 + z_lo), core: 2. Of those that a mesh axis runs over, the one named last changes fastest.
Arguments:
- coupling: float32 [128, 1024, 1024], P('tm', 'rows'), may hold values from -0.078125 to 0.078125
- field: float32 [128, 1024], P('tm', 'rows'), may hold values from -1.2 to 1.2
Outputs:
- reduced: float32 [128, 1024, 1024], P('tm', 'rows')
The draws below stay inside these ranges and needn't reach their ends.
All inputs are finite; a program needn't handle non-finite values.
Results may differ from the reference program's by a relative error of at most 0.00015.
Values sent between devices are 32-bit elements; how exact they have to be, the bound alone decides.
A program may use at most 64 MiB of HBM per device.

```python
import jax
import jax.numpy as jnp
from jax import lax

NS = 1024
NB = 128


def shard_levels(key, shape, pieces, least, top_value):
    gain = 1.0
    for dim, parts in pieces:
        heights = jax.random.uniform(jax.random.fold_in(jax.random.fold_in(key, 6), dim), (parts,), jnp.float32, least / len(pieces), top_value / len(pieces))
        gain = gain * jnp.repeat(jnp.exp(heights), shape[dim] // parts).reshape((-1,) + (1,) * (len(shape) - 1 - dim))
    return gain


def noise(rng, extent, width, reach, split=(), held_as=jnp.bfloat16):
    entries = jax.random.normal(rng, extent, jnp.float32) * width
    if len(split) > 0:
        entries = shard_levels(rng, extent, split, -0.22, 0.18) * entries
    return jnp.clip(entries, min=-reach, max=reach).astype(held_as)


def setup_inputs(seed: int = 0) -> dict:
    streams_of = jax.random.split(jax.random.key(seed), 3)
    return {
        "coupling": noise(streams_of[0], (NB, NS, NS), (6 * NS) ** -0.5, 0.078125, ((0, 128), (1, 4)), jnp.float32),
        "field": noise(streams_of[1], (NB, NS), 0.3, 1.2, ((0, 128), (1, 4)), jnp.float32),
    }


def reference(coupling, field):
    eye = jnp.eye(NS, dtype=jnp.float32)
    block = jnp.exp(field)[:, :, None] * (eye[None] + coupling)

    def mult(pair):
        return jnp.matmul(pair[0], pair[1], precision=lax.Precision.HIGHEST)

    paired = lax.map(mult, (jnp.roll(block, -1, axis=0), block))
    return lax.map(mult, (jnp.roll(paired, -2, axis=0), paired))
```

```python
import functools

import jax
import jax.numpy as jnp
from jax import lax
from jax.experimental import pallas as pl
from jax.experimental.pallas import tpu as pltpu
from jax.sharding import PartitionSpec as P

F32 = jnp.float32
BF16 = jnp.bfloat16
MESH = pl.DeviceIdType.MESH

WIDE = 128
AHEAD = 2
START = 6


def split(x):
    hi = x.astype(BF16)
    return hi, (x - hi.astype(F32)).astype(BF16)


def dot3(ah, al, bh, bl):
    def mm(a, b):
        return jnp.dot(a, b, preferred_element_type=F32)

    return mm(ah, bh) + (mm(ah, bl) + mm(al, bh))


def kernel(
    n_t, n_r, coupling, field, out,
    raw, full, sib, rowbuf, lhs_h, lhs_l, own_h, own_l, one_h, one_l,
    stage_a, stage_b, land_a, land_b, acc, res,
    local_sem, out_sem,
    own_s, own_r, fwd_s, fwd_r, sib_s, sib_r, xo_s, xo_r, row_s, row_r, a_s, a_r, b_s, b_r,
):
    t = lax.axis_index("tm")
    r = lax.axis_index("rows")
    rows = raw.shape[0]
    nch = full.shape[0]
    even = lax.rem(t, 2) == 0
    half = rows // 2

    def tm(by):
        return lax.rem(t + by + n_t, n_t)

    def at_t(by):
        return (tm(by), r)

    def at_r(by):
        return (t, lax.rem(r + by + n_r, n_r))

    def plane(by):
        return pl.multiple_of(lax.rem(r + by + n_r, n_r) * rows, rows)

    load = pltpu.make_async_copy(coupling.at[0], raw, local_sem)
    load.start()

    barrier = pltpu.get_barrier_semaphore()
    for by in (1, -1):
        pl.semaphore_signal(barrier, inc=1, device_id=at_r(by), device_id_type=MESH)
    pl.semaphore_signal(barrier, inc=1, device_id=at_t(1), device_id_type=MESH)

    @pl.when(even)
    def _():
        pl.semaphore_signal(barrier, inc=1, device_id=at_t(2), device_id_type=MESH)

    def copy(src, dst, ssem, rsem, dev):
        return pltpu.make_async_remote_copy(
            src_ref=src, dst_ref=dst, send_sem=ssem, recv_sem=rsem,
            device_id=dev, device_id_type=MESH,
        )

    def own(c, d):
        piece = full.at[c, pl.ds(plane(0), rows), :]
        return copy(piece, piece, own_s.at[d, c], own_r.at[d, c], at_r(1 - 2 * d))

    def own_in(c, d):
        piece = full.at[c, pl.ds(plane(2 * d - 1), rows), :]
        return copy(piece, piece, own_s.at[d, c], own_r.at[d, c], at_r(1 - 2 * d))

    def fwd(c, d):
        piece = full.at[c, pl.ds(pl.multiple_of(plane(2 * d - 1) + d * half, half), half), :]
        return copy(piece, piece, fwd_s.at[d, c], fwd_r.at[d, c], at_r(1 - 2 * d))

    def fwd_in(c, d):
        piece = full.at[c, pl.ds(pl.multiple_of(plane(2) + d * half, half), half), :]
        return copy(piece, piece, fwd_s.at[d, c], fwd_r.at[d, c], at_r(1 - 2 * d))

    def to_sib(c):
        return copy(full.at[c], sib.at[c], sib_s.at[c], sib_r.at[c], at_t(-1))

    def xo(c):
        return copy(stage_a.at[c], land_a.at[c], xo_s.at[c], xo_r.at[c], at_t(-1))

    def row():
        return copy(full.at[:, pl.ds(plane(0), rows), :], rowbuf, row_s, row_r, at_t(-1))

    def send_a(c):
        return copy(stage_a.at[c], land_b.at[c], a_s.at[c], a_r.at[c], at_t(-2))

    def send_b(c):
        return copy(stage_b.at[c], land_b.at[c], b_s.at[c], b_r.at[c], at_t(-1))

    def cols(c):
        return pl.ds(pl.multiple_of(c * WIDE, WIDE), WIDE)

    scale = jnp.exp(jnp.transpose(jnp.broadcast_to(field[...], (WIDE, rows))))
    load.wait()
    row_ids = lax.broadcasted_iota(jnp.int32, (rows, WIDE), 0) + r * rows
    col_ids = lax.broadcasted_iota(jnp.int32, (rows, WIDE), 1)

    def build(c, _):
        ident = jnp.where(row_ids == col_ids + c * WIDE, 1.0, 0.0).astype(F32)
        full[c, pl.ds(plane(0), rows), :] = scale * (ident + raw[:, cols(c)])
        return 0

    lax.fori_loop(0, nch, build, 0)

    def gather(process):
        for c in range(AHEAD):
            for d in (0, 1):
                own(c, d).start()

        def step(c, _):
            @pl.when(c < nch)
            def _():
                for d in (0, 1):
                    own_in(c, d).wait_recv()
                    fwd(c, d).start()

            @pl.when(c + AHEAD < nch)
            def _():
                for d in (0, 1):
                    own(c + AHEAD, d).start()

            @pl.when(c >= 1)
            def _():
                for d in (0, 1):
                    fwd_in(c - 1, d).wait_recv()
                process(c - 1)

            return 0

        lax.fori_loop(0, nch + 1, step, 0)

    def drain(c, _):
        for d in (0, 1):
            own(c, d).wait_send()
            fwd(c, d).wait_send()
        return 0

    def fill_lhs(c, first):
        hi, lo = split(rowbuf[c])
        lhs_h[first : first + rows, cols(c)] = hi
        lhs_l[first : first + rows, cols(c)] = lo

    def add_chunk(c, land, total):
        h, l = split(land[c])
        total[...] += dot3(h, l, one_h[cols(c), :], one_l[cols(c), :])

    @pl.when(jnp.logical_not(even))
    def _():
        pl.semaphore_wait(barrier, 3)
        row().start()

        def left_factor():
            row().wait_recv()

            def body(c, _):
                fill_lhs(c, 0)
                return 0

            lax.fori_loop(0, nch, body, 0)

        def product(c):
            stage_a[c] = dot3(
                lhs_h[0:rows, :], lhs_l[0:rows, :], one_h[:, cols(c)], one_l[:, cols(c)]
            )
            xo(c).start()

        lag = 3

        def process(c):
            to_sib(c).start()
            hi, lo = split(full[c])
            one_h[:, cols(c)] = hi
            one_l[:, cols(c)] = lo

            @pl.when(c == lag)
            def _():
                left_factor()

            @pl.when(c >= lag)
            def _():
                product(c - lag)

        gather(process)

        def rest(c, _):
            product(c)
            return 0

        lax.fori_loop(nch - lag, nch, rest, 0)

        acc[...] = jnp.zeros_like(acc)

        def body(c, _):
            send_b(c).wait_recv()
            add_chunk(c, land_b, acc)
            return 0

        lax.fori_loop(0, nch, body, 0)
        write = pltpu.make_async_copy(acc, out.at[0], out_sem.at[0])
        write.start()
        row().wait_send()

        def finish(c, _):
            to_sib(c).wait_send()
            xo(c).wait_send()
            return 0

        lax.fori_loop(0, nch, finish, 0)
        lax.fori_loop(0, nch, drain, 0)
        write.wait()

    @pl.when(even)
    def _():
        pl.semaphore_wait(barrier, 4)
        row().start()
        row().wait_recv()

        def fill(c, _):
            fill_lhs(c, 0)
            return 0

        lax.fori_loop(0, nch, fill, 0)

        def take(c, _):
            to_sib(c).wait_recv()
            hi, lo = split(sib[c])
            one_h[:, cols(c)] = hi
            one_l[:, cols(c)] = lo
            return 0

        lax.fori_loop(0, START, take, 0)
        acc[...] = jnp.zeros_like(acc)
        lag = 2

        def process(c):
            @pl.when(c == 0)
            def _():
                lax.fori_loop(START, nch, take, 0)

                def body(k, _):
                    xo(k).wait_recv()
                    hi, lo = split(land_a[k])
                    lhs_h[rows : 2 * rows, cols(k)] = hi
                    lhs_l[rows : 2 * rows, cols(k)] = lo
                    return 0

                lax.fori_loop(0, nch, body, 0)

            bh, bl = split(full[c])
            own_h[:, cols(c)] = bh
            own_l[:, cols(c)] = bl
            y = dot3(lhs_h[...], lhs_l[...], bh, bl)
            stage_a[c] = y[0:rows]
            send_a(c).start()
            stage_b[c] = y[rows:]
            send_b(c).start()

            @pl.when(c >= lag)
            def _():
                send_a(c - lag).wait_recv()
                add_chunk(c - lag, land_b, acc)

        gather(process)

        def rest(c, _):
            send_a(c).wait_recv()
            add_chunk(c, land_b, acc)
            return 0

        lax.fori_loop(nch - lag, nch, rest, 0)

        xh, xl = split(acc[...])
        wide = 2 * WIDE
        for k in range(nch // 2):
            part = slice(k * wide, (k + 1) * wide)
            res[k] = dot3(xh, xl, own_h[:, part], own_l[:, part])
            pltpu.make_async_copy(res.at[k], out.at[0, :, part], out_sem.at[k]).start()
        row().wait_send()

        def finish(c, _):
            send_a(c).wait_send()
            send_b(c).wait_send()
            return 0

        lax.fori_loop(0, nch, finish, 0)
        lax.fori_loop(0, nch, drain, 0)
        for k in range(nch // 2):
            part = slice(k * wide, (k + 1) * wide)
            pltpu.make_async_copy(res.at[k], out.at[0, :, part], out_sem.at[k]).wait()


def per_device(n_t, n_r, coupling, field):
    _, rows, sites = coupling.shape
    nch = sites // WIDE
    dma = pltpu.SemaphoreType.DMA
    piece = pltpu.VMEM((nch, rows, WIDE), F32)
    whole = pltpu.VMEM((nch, sites, WIDE), F32)
    return pl.pallas_call(
        functools.partial(kernel, n_t, n_r),
        out_shape=jax.ShapeDtypeStruct((1, rows, sites), F32),
        in_specs=[
            pl.BlockSpec(memory_space=pl.ANY),
            pl.BlockSpec(memory_space=pltpu.VMEM),
        ],
        out_specs=pl.BlockSpec(memory_space=pl.ANY),
        scratch_shapes=[
            pltpu.VMEM((rows, sites), F32),
            whole,
            whole,
            piece,
            pltpu.VMEM((2 * rows, sites), BF16),
            pltpu.VMEM((2 * rows, sites), BF16),
            pltpu.VMEM((sites, sites), BF16),
            pltpu.VMEM((sites, sites), BF16),
            pltpu.VMEM((sites, sites), BF16),
            pltpu.VMEM((sites, sites), BF16),
            piece,
            piece,
            piece,
            piece,
            pltpu.VMEM((rows, sites), F32),
            pltpu.VMEM((nch // 2, rows, 2 * WIDE), F32),
            dma,
            dma((nch,)),
            dma((2, nch)),
            dma((2, nch)),
            dma((2, nch)),
            dma((2, nch)),
            dma((nch,)),
            dma((nch,)),
            dma((nch,)),
            dma((nch,)),
            dma,
            dma,
            dma((nch,)),
            dma((nch,)),
            dma((nch,)),
            dma((nch,)),
        ],
        compiler_params=pltpu.CompilerParams(
            collective_id=0, has_side_effects=True, vmem_limit_bytes=56 * 2**20
        ),
        cost_estimate=pl.CostEstimate(
            flops=18 * rows * sites * sites, bytes_accessed=8 * rows * sites, transcendentals=0
        ),
    )(coupling, field)


def solution(mesh):
    return jax.shard_map(
        functools.partial(per_device, mesh.shape["tm"], mesh.shape["rows"]),
        mesh=mesh,
        in_specs=(P("tm", "rows", None), P("tm", "rows")),
        out_specs=P("tm", "rows", None),
        check_vma=False,
    )
```

```python
import functools

import jax
import jax.numpy as jnp
from jax import lax
from jax.experimental import pallas as pl
from jax.experimental.pallas import tpu as pltpu
from jax.sharding import PartitionSpec as P

F32 = jnp.float32
BF16 = jnp.bfloat16
MESH = pl.DeviceIdType.MESH

WIDE = 128
AHEAD = 2
START = 5


def split(x):
    hi = x.astype(BF16)
    return hi, (x - hi.astype(F32)).astype(BF16)


def dot3(ah, al, bh, bl):
    def mm(a, b):
        return jnp.dot(a, b, preferred_element_type=F32)

    return mm(ah, bh) + (mm(ah, bl) + mm(al, bh))


def kernel(
    n_t, n_r, coupling, field, out,
    raw, full, sib, rowbuf, lhs_h, lhs_l, own_h, own_l, one_h, one_l,
    stage_a, stage_b, land_a, land_b, acc, res, meet_h, meet_l,
    rel, local_sem, out_sem, rel_s, rel_r,
    own_s, own_r, fwd_s, fwd_r, sib_s, sib_r, xo_s, xo_r, row_s, row_r, a_s, a_r, b_s, b_r,
):
    t = lax.axis_index("tm")
    r = lax.axis_index("rows")
    rows = raw.shape[0]
    nch = full.shape[0]
    even = lax.rem(t, 2) == 0
    half = rows // 2
    span = n_t // 2
    place = lax.rem(t, span)
    base = t - place
    other = span - base
    line = 16
    n_rel = nch - 1
    odd = jnp.logical_not(even)
    is_src = place == 0
    is_dst = place >= span - 2
    kind = place // line - 1
    mine = lax.rem(place, line) // 2
    is_rel = jnp.logical_and(
        jnp.logical_and(kind >= 0, mine < n_rel),
        jnp.logical_or(jnp.logical_and(even, kind == 0), jnp.logical_and(odd, kind > 0)),
    )

    def way(k, c):
        return (k + 1) * line + 2 * c + (1 if k else 0)

    def tm(by):
        return lax.rem(t + by + n_t, n_t)

    def at_t(by):
        return (tm(by), r)

    def at_r(by):
        return (t, lax.rem(r + by + n_r, n_r))

    def plane(by):
        return pl.multiple_of(lax.rem(r + by + n_r, n_r) * rows, rows)

    def load(c):
        return pltpu.make_async_copy(
            coupling.at[0, :, cols(c)], raw.at[:, cols(c)], local_sem.at[c]
        )

    def cols(c):
        return pl.ds(pl.multiple_of(c * WIDE, WIDE), WIDE)

    for c in range(nch):
        load(c).start()

    barrier = pltpu.get_barrier_semaphore()
    for by in (1, -1):
        pl.semaphore_signal(barrier, inc=1, device_id=at_r(by), device_id_type=MESH)
    pl.semaphore_signal(barrier, inc=1, device_id=at_t(1), device_id_type=MESH)

    @pl.when(even)
    def _():
        pl.semaphore_signal(barrier, inc=1, device_id=at_t(2), device_id_type=MESH)

    @pl.when(is_rel)
    def _():
        for to in (base, other + place):
            pl.semaphore_signal(barrier, inc=1, device_id=(to, r), device_id_type=MESH)

    def greet(k):
        for c in range(n_rel):
            to = (base + way(k, c), r)
            pl.semaphore_signal(barrier, inc=1, device_id=to, device_id_type=MESH)

    @pl.when(jnp.logical_and(is_dst, even))
    def _():
        greet(1)

    @pl.when(jnp.logical_and(is_dst, odd))
    def _():
        greet(0)
        greet(2)

    def copy(src, dst, ssem, rsem, dev):
        return pltpu.make_async_remote_copy(
            src_ref=src, dst_ref=dst, send_sem=ssem, recv_sem=rsem,
            device_id=dev, device_id_type=MESH,
        )

    def own(c, d):
        piece = full.at[c, pl.ds(plane(0), rows), :]
        return copy(piece, piece, own_s.at[d, c], own_r.at[d, c], at_r(1 - 2 * d))

    def own_in(c, d):
        piece = full.at[c, pl.ds(plane(2 * d - 1), rows), :]
        return copy(piece, piece, own_s.at[d, c], own_r.at[d, c], at_r(1 - 2 * d))

    def fwd(c, d):
        piece = full.at[c, pl.ds(pl.multiple_of(plane(2 * d - 1) + d * half, half), half), :]
        return copy(piece, piece, fwd_s.at[d, c], fwd_r.at[d, c], at_r(1 - 2 * d))

    def fwd_in(c, d):
        piece = full.at[c, pl.ds(pl.multiple_of(plane(2) + d * half, half), half), :]
        return copy(piece, piece, fwd_s.at[d, c], fwd_r.at[d, c], at_r(1 - 2 * d))

    def to_sib(c):
        return copy(full.at[c], sib.at[c], sib_s.at[c], sib_r.at[c], at_t(-1))

    def xo(c):
        return copy(stage_a.at[c], land_a.at[c], xo_s.at[c], xo_r.at[c], at_t(-1))

    def row(c):
        piece = full.at[c, pl.ds(plane(0), rows), :]
        return copy(piece, rowbuf.at[c], row_s.at[c], row_r.at[c], at_t(-1))

    def send_a(c):
        return copy(stage_a.at[c], land_b.at[c], a_s.at[c], a_r.at[c], at_t(-2))

    def send_b(c):
        return copy(stage_b.at[c], land_b.at[c], b_s.at[c], b_r.at[c], at_t(-1))

    def by_way(k, c):
        src = (full.at[c, pl.ds(plane(0), rows), :], stage_a.at[c], stage_b.at[c])[k]
        sem = (row_s, a_s, b_s)[k].at[c]
        return copy(src, rel.at[0], sem, rel_r.at[0], (base + way(k, c), r))

    def start(k, c):
        go = (row, send_a, send_b)[k]
        by = jnp.logical_and(is_src, c < n_rel)

        @pl.when(by)
        def _():
            by_way(k, c).start()

        @pl.when(jnp.logical_not(by))
        def _():
            go(c).start()

    def over():
        return copy(rel.at[0], rel.at[1], rel_s.at[0], rel_r.at[1], (other + place, r))

    def last_leg(k):
        dst, sem, back = ((rowbuf, row_r, 1), (land_b, a_r, 2), (land_b, b_r, 1))[k]
        to = (lax.rem(other - back + n_t, n_t), r)
        return copy(rel.at[1], dst.at[mine], rel_s.at[1], sem.at[mine], to)

    def hand_on(kinds):
        @pl.when(is_rel)
        def _():
            copy(rel.at[0], rel.at[0], rel_s.at[0], rel_r.at[0], (base, r)).wait_recv()
            over().start()
            over().wait_recv()

        for k in kinds:

            @pl.when(jnp.logical_and(is_rel, kind == k))
            def _():
                last_leg(k).start()

    def handed(kinds):
        for k in kinds:

            @pl.when(jnp.logical_and(is_rel, kind == k))
            def _():
                over().wait_send()
                last_leg(k).wait_send()

    scale = jnp.exp(jnp.transpose(jnp.broadcast_to(field[...], (WIDE, rows))))
    row_ids = lax.broadcasted_iota(jnp.int32, (rows, WIDE), 0) + r * rows
    col_ids = lax.broadcasted_iota(jnp.int32, (rows, WIDE), 1)

    def build(c, _):
        load(c).wait()
        ident = jnp.where(row_ids == col_ids + c * WIDE, 1.0, 0.0).astype(F32)
        full[c, pl.ds(plane(0), rows), :] = scale * (ident + raw[:, cols(c)])
        return 0

    lax.fori_loop(0, AHEAD, build, 0)

    def rest_of_block():
        lax.fori_loop(AHEAD, nch, build, 0)

        def send(c, _):
            start(0, c)

            @pl.when(is_src)
            def _():
                row(c).wait_send()

            return 0

        lax.fori_loop(0, nch, send, 0)

    def gather(process, before):
        for c in range(AHEAD):
            for d in (0, 1):
                own(c, d).start()
        before()

        def step(c, _):
            @pl.when(c < nch)
            def _():
                for d in (0, 1):
                    own_in(c, d).wait_recv()
                    fwd(c, d).start()

            @pl.when(c + AHEAD < nch)
            def _():
                for d in (0, 1):
                    own(c + AHEAD, d).start()

            @pl.when(c >= 1)
            def _():
                for d in (0, 1):
                    fwd_in(c - 1, d).wait_recv()
                process(c - 1)

            return 0

        lax.fori_loop(0, nch + 1, step, 0)

    def drain(c, _):
        for d in (0, 1):
            own(c, d).wait_send()
            fwd(c, d).wait_send()
        return 0

    def fill_lhs(c, first):
        hi, lo = split(rowbuf[c])
        lhs_h[first : first + rows, cols(c)] = hi
        lhs_l[first : first + rows, cols(c)] = lo

    def add_chunk(c, land, total):
        h, l = split(land[c])
        total[...] += dot3(h, l, one_h[cols(c), :], one_l[cols(c), :])

    @pl.when(jnp.logical_not(even))
    def _():
        pl.semaphore_wait(barrier, jnp.where(is_rel, 5, 3))

        def left_factor():
            def body(c, _):
                row(c).wait_recv()
                fill_lhs(c, 0)
                return 0

            lax.fori_loop(0, nch, body, 0)

        def product(c, _):
            stage_a[c] = dot3(
                lhs_h[0:rows, :], lhs_l[0:rows, :], one_h[:, cols(c)], one_l[:, cols(c)]
            )
            xo(c).start()
            return 0

        lag = 5

        def process(c):
            to_sib(c).start()
            hi, lo = split(full[c])
            one_h[:, cols(c)] = hi
            one_l[:, cols(c)] = lo

            @pl.when(c == lag)
            def _():
                left_factor()
                lax.fori_loop(0, lag, product, 0)

            @pl.when(c >= lag)
            def _():
                product(c, 0)

        gather(process, rest_of_block)
        acc[...] = jnp.zeros_like(acc)

        def body(c, _):
            @pl.when(c == mine)
            def _():
                hand_on((1, 2))

            send_b(c).wait_recv()
            add_chunk(c, land_b, acc)
            return 0

        lax.fori_loop(0, nch, body, 0)
        write = pltpu.make_async_copy(acc, out.at[0], out_sem.at[0])
        write.start()

        def finish(c, _):
            row(c).wait_send()
            to_sib(c).wait_send()
            xo(c).wait_send()
            return 0

        lax.fori_loop(0, nch, finish, 0)
        lax.fori_loop(0, nch, drain, 0)

        handed((1, 2))
        write.wait()

    @pl.when(even)
    def _():
        pl.semaphore_wait(barrier, jnp.where(is_src, 4 + 3 * n_rel, jnp.where(is_rel, 6, 4)))
        rest_of_block()

        hand_on((0,))

        def fill(c, _):
            row(c).wait_recv()
            fill_lhs(c, 0)
            return 0

        lax.fori_loop(0, nch, fill, 0)

        def take(c, _):
            to_sib(c).wait_recv()
            hi, lo = split(sib[c])
            one_h[:, cols(c)] = hi
            one_l[:, cols(c)] = lo
            return 0

        lax.fori_loop(0, START, take, 0)
        def process(c):
            @pl.when(c == 0)
            def _():
                lax.fori_loop(START, nch, take, 0)

                def body(k, _):
                    xo(k).wait_recv()
                    hi, lo = split(land_a[k])
                    lhs_h[rows : 2 * rows, cols(k)] = hi
                    lhs_l[rows : 2 * rows, cols(k)] = lo
                    return 0

                lax.fori_loop(0, nch, body, 0)

            bh, bl = split(full[c])
            own_h[:, cols(c)] = bh
            own_l[:, cols(c)] = bl
            y = dot3(lhs_h[...], lhs_l[...], bh, bl)
            stage_a[c] = y[0:rows]
            start(1, c)
            stage_b[c] = y[rows:]
            start(2, c)

        gather(process, lambda: None)

        def collect(c, _):
            send_a(c).wait_recv()
            hi, lo = split(land_b[c])
            lhs_h[0:rows, cols(c)] = hi
            lhs_l[0:rows, cols(c)] = lo
            return 0

        lax.fori_loop(0, nch - 1, collect, 0)

        cut = (nch - 1) * WIDE
        wide = 2 * WIDE
        parts = [slice(k * wide, (k + 1) * wide) for k in range(nch // 2)]
        fh, fl = lhs_h[0:rows, 0:cut], lhs_l[0:rows, 0:cut]
        for part in parts:
            x = dot3(fh, fl, one_h[0:cut, part], one_l[0:cut, part])
            lhs_h[rows:, part], lhs_l[rows:, part] = split(x)
        xh, xl = lhs_h[rows:, :], lhs_l[rows:, :]
        gh, gl = one_h[cut:, :], one_l[cut:, :]
        for k, part in enumerate(parts):
            vh, vl = own_h[:, part], own_l[:, part]
            res[k] = dot3(xh, xl, vh, vl)
            meet_h[:, part], meet_l[:, part] = split(dot3(gh, gl, vh, vl))

        send_a(nch - 1).wait_recv()
        lh, ll = split(land_b[nch - 1])
        for k, part in enumerate(parts):
            res[k] += dot3(lh, ll, meet_h[:, part], meet_l[:, part])
            pltpu.make_async_copy(res.at[k], out.at[0, :, part], out_sem.at[k]).start()

        def finish(c, _):
            @pl.when(jnp.logical_not(is_src))
            def _():
                row(c).wait_send()

            send_a(c).wait_send()
            send_b(c).wait_send()
            return 0

        lax.fori_loop(0, nch, finish, 0)
        lax.fori_loop(0, nch, drain, 0)

        handed((0,))
        for k, part in enumerate(parts):
            pltpu.make_async_copy(res.at[k], out.at[0, :, part], out_sem.at[k]).wait()


def per_device(n_t, n_r, coupling, field):
    _, rows, sites = coupling.shape
    nch = sites // WIDE
    dma = pltpu.SemaphoreType.DMA
    piece = pltpu.VMEM((nch, rows, WIDE), F32)
    whole = pltpu.VMEM((nch, sites, WIDE), F32)
    return pl.pallas_call(
        functools.partial(kernel, n_t, n_r),
        out_shape=jax.ShapeDtypeStruct((1, rows, sites), F32),
        in_specs=[
            pl.BlockSpec(memory_space=pl.ANY),
            pl.BlockSpec(memory_space=pltpu.VMEM),
        ],
        out_specs=pl.BlockSpec(memory_space=pl.ANY),
        scratch_shapes=[
            pltpu.VMEM((rows, sites), F32),
            whole,
            whole,
            piece,
            pltpu.VMEM((2 * rows, sites), BF16),
            pltpu.VMEM((2 * rows, sites), BF16),
            pltpu.VMEM((sites, sites), BF16),
            pltpu.VMEM((sites, sites), BF16),
            pltpu.VMEM((sites, sites), BF16),
            pltpu.VMEM((sites, sites), BF16),
            piece,
            piece,
            piece,
            piece,
            pltpu.VMEM((rows, sites), F32),
            pltpu.VMEM((nch // 2, rows, 2 * WIDE), F32),
            pltpu.VMEM((WIDE, sites), BF16),
            pltpu.VMEM((WIDE, sites), BF16),
            pltpu.VMEM((2, rows, WIDE), F32),
            dma((nch,)),
            dma((nch,)),
            dma((2,)),
            dma((2,)),
            dma((2, nch)),
            dma((2, nch)),
            dma((2, nch)),
            dma((2, nch)),
            dma((nch,)),
            dma((nch,)),
            dma((nch,)),
            dma((nch,)),
            dma((nch,)),
            dma((nch,)),
            dma((nch,)),
            dma((nch,)),
            dma((nch,)),
            dma((nch,)),
        ],
        compiler_params=pltpu.CompilerParams(
            collective_id=0, has_side_effects=True, vmem_limit_bytes=56 * 2**20
        ),
        cost_estimate=pl.CostEstimate(
            flops=18 * rows * sites * sites, bytes_accessed=8 * rows * sites, transcendentals=0
        ),
    )(coupling, field)


def solution(mesh):
    return jax.shard_map(
        functools.partial(per_device, mesh.shape["tm"], mesh.shape["rows"]),
        mesh=mesh,
        in_specs=(P("tm", "rows", None), P("tm", "rows")),
        out_specs=P("tm", "rows", None),
        check_vma=False,
    )
```

```python
import functools

import jax
import jax.numpy as jnp
from jax import lax
from jax.experimental import pallas as pl
from jax.experimental.pallas import tpu as pltpu
from jax.sharding import PartitionSpec as P

F32 = jnp.float32
BF16 = jnp.bfloat16
MESH = pl.DeviceIdType.MESH

WIDE = 128
AHEAD = 2
FOLD = 2
LEAD = 1
START = 5


def split(x):
    hi = x.astype(BF16)
    return hi, (x - hi.astype(F32)).astype(BF16)


def dot3(ah, al, bh, bl):
    def mm(a, b):
        return jnp.dot(a, b, preferred_element_type=F32)

    return mm(ah, bh) + (mm(ah, bl) + mm(al, bh))


def kernel(
    n_t, n_r, coupling, field, out,
    full, sib, rowbuf, lhs_h, lhs_l, own_h, own_l, one_h, one_l,
    stage_a, stage_b, land_a, land_b, meet_h, meet_l,
    rel, pace, rel_s, rel_r,
    own_s, own_r, fwd_s, fwd_r, sib_s, sib_r, xo_s, xo_r, row_s, row_r, a_s, a_r, b_s, b_r,
):
    t = lax.axis_index("tm")
    r = lax.axis_index("rows")
    rows = coupling.shape[1]
    nch = full.shape[0]
    even = lax.rem(t, 2) == 0
    half = rows // 2
    span = n_t // 2
    place = lax.rem(t, span)
    base = t - place
    other = span - base
    line = 16
    n_rel = (nch, nch - 1, nch - 1)
    odd = jnp.logical_not(even)
    is_src = place == 0
    is_dst = place >= span - 2
    kind = place // line - 1
    mine = lax.rem(place, line) // 2
    is_rel = jnp.logical_or(
        jnp.logical_and(even, kind == 0),
        jnp.logical_and(odd, jnp.logical_and(kind > 0, mine < n_rel[1])),
    )

    def way(k, c):
        return (k + 1) * line + 2 * c + (1 if k else 0)

    def tm(by):
        return lax.rem(t + by + n_t, n_t)

    def at_t(by):
        return (tm(by), r)

    def at_r(by):
        return (t, lax.rem(r + by + n_r, n_r))

    def plane(by):
        return pl.multiple_of(lax.rem(r + by + n_r, n_r) * rows, rows)

    def cols(c):
        return pl.ds(pl.multiple_of(c * WIDE, WIDE), WIDE)

    barrier = pltpu.get_barrier_semaphore()
    for by in (1, -1):
        pl.semaphore_signal(barrier, inc=1, device_id=at_r(by), device_id_type=MESH)
    pl.semaphore_signal(barrier, inc=1, device_id=at_t(1), device_id_type=MESH)

    @pl.when(even)
    def _():
        pl.semaphore_signal(barrier, inc=1, device_id=at_t(2), device_id_type=MESH)

    @pl.when(is_rel)
    def _():
        for to in (base, other + place):
            pl.semaphore_signal(barrier, inc=1, device_id=(to, r), device_id_type=MESH)

    beside = (other + place, r)
    pl.semaphore_signal(barrier, inc=1, device_id=beside, device_id_type=MESH)

    def greet(k):
        for c in range(n_rel[k]):
            to = (base + way(k, c), r)
            pl.semaphore_signal(barrier, inc=1, device_id=to, device_id_type=MESH)

    @pl.when(jnp.logical_and(is_dst, even))
    def _():
        greet(1)

    @pl.when(jnp.logical_and(is_dst, odd))
    def _():
        greet(0)
        greet(2)

    def copy(src, dst, ssem, rsem, dev):
        return pltpu.make_async_remote_copy(
            src_ref=src, dst_ref=dst, send_sem=ssem, recv_sem=rsem,
            device_id=dev, device_id_type=MESH,
        )

    def own(c, d):
        piece = full.at[c, pl.ds(plane(0), rows), :]
        return copy(piece, piece, own_s.at[d, c], own_r.at[d, c], at_r(1 - 2 * d))

    def own_in(c, d):
        piece = full.at[c, pl.ds(plane(2 * d - 1), rows), :]
        return copy(piece, piece, own_s.at[d, c], own_r.at[d, c], at_r(1 - 2 * d))

    def fwd(c, d):
        piece = full.at[c, pl.ds(pl.multiple_of(plane(2 * d - 1) + d * half, half), half), :]
        return copy(piece, piece, fwd_s.at[d, c], fwd_r.at[d, c], at_r(1 - 2 * d))

    def fwd_in(c, d):
        piece = full.at[c, pl.ds(pl.multiple_of(plane(2) + d * half, half), half), :]
        return copy(piece, piece, fwd_s.at[d, c], fwd_r.at[d, c], at_r(1 - 2 * d))

    def to_sib(c):
        return copy(full.at[c], sib.at[c], sib_s.at[c], sib_r.at[c], at_t(-1))

    def xo(c):
        return copy(stage_a.at[c], land_a.at[c], xo_s.at[c], xo_r.at[c], at_t(-1))

    def row(c):
        piece = full.at[c, pl.ds(plane(0), rows), :]
        return copy(piece, rowbuf.at[c], row_s.at[c], row_r.at[c], at_t(-1))

    def send_a(c):
        return copy(stage_a.at[c], land_b.at[c], a_s.at[c], a_r.at[c], at_t(-2))

    def send_b(c):
        return copy(stage_b.at[c], land_b.at[c], b_s.at[c], b_r.at[c], at_t(-1))

    def by_way(k, c):
        src = (full.at[c, pl.ds(plane(0), rows), :], stage_a.at[c], stage_b.at[c])[k]
        sem = (row_s, a_s, b_s)[k].at[c]
        return copy(src, rel.at[0], sem, rel_r.at[0], (base + way(k, c), r))

    def start(k, c):
        go = (row, send_a, send_b)[k]
        by = jnp.logical_and(is_src, c < n_rel[k])

        @pl.when(by)
        def _():
            by_way(k, c).start()

        @pl.when(jnp.logical_not(by))
        def _():
            go(c).start()

    def over():
        return copy(rel.at[0], rel.at[1], rel_s.at[0], rel_r.at[1], (other + place, r))

    def last_leg(k):
        dst, sem, back = ((rowbuf, row_r, 1), (land_b, a_r, 2), (land_b, b_r, 1))[k]
        to = (lax.rem(other - back + n_t, n_t), r)
        return copy(rel.at[1], dst.at[mine], rel_s.at[1], sem.at[mine], to)

    def hand_on(kinds):
        @pl.when(is_rel)
        def _():
            copy(rel.at[0], rel.at[0], rel_s.at[0], rel_r.at[0], (base, r)).wait_recv()
            over().start()
            over().wait_recv()

        for k in kinds:

            @pl.when(jnp.logical_and(is_rel, kind == k))
            def _():
                last_leg(k).start()

    def handed(kinds):
        for k in kinds:

            @pl.when(jnp.logical_and(is_rel, kind == k))
            def _():
                over().wait_send()
                last_leg(k).wait_send()

    scale = jnp.exp(jnp.transpose(jnp.broadcast_to(field[...], (WIDE, rows))))
    row_ids = lax.broadcasted_iota(jnp.int32, (rows, WIDE), 0) + r * rows
    col_ids = lax.broadcasted_iota(jnp.int32, (rows, WIDE), 1)

    def build(c, _):
        ident = jnp.where(row_ids == col_ids + c * WIDE, 1.0, 0.0).astype(F32)
        full[c, pl.ds(plane(0), rows), :] = scale * (ident + coupling[0, :, cols(c)])
        return 0

    lax.fori_loop(0, AHEAD, build, 0)

    def rest_of_block():
        lax.fori_loop(AHEAD, nch, build, 0)

        def send(c, _):
            start(0, c)

            @pl.when(is_src)
            def _():
                row(c).wait_send()

            return 0

        lax.fori_loop(0, nch, send, 0)

    def gather(process, before):
        for c in range(AHEAD):
            for d in (0, 1):
                own(c, d).start()
        before()

        def step(c, _):
            @pl.when(c < nch)
            def _():
                for d in (0, 1):
                    own_in(c, d).wait_recv()
                    fwd(c, d).start()

            @pl.when(c + AHEAD + LEAD < nch)
            def _():
                pl.semaphore_signal(pace, inc=1, device_id=beside, device_id_type=MESH)

            @pl.when(c + AHEAD < nch)
            def _():
                @pl.when(c >= LEAD)
                def _():
                    pl.semaphore_wait(pace, 1)

                for d in (0, 1):
                    own(c + AHEAD, d).start()

            @pl.when(c >= 1)
            def _():
                for d in (0, 1):
                    fwd_in(c - 1, d).wait_recv()
                process(c - 1)

            return 0

        lax.fori_loop(0, nch + 1, step, 0)

    def drain(c, _):
        for d in (0, 1):
            own(c, d).wait_send()
            fwd(c, d).wait_send()
        return 0

    def fill_lhs(c, first):
        hi, lo = split(rowbuf[c])
        lhs_h[first : first + rows, cols(c)] = hi
        lhs_l[first : first + rows, cols(c)] = lo

    def add_chunk(c):
        h, l = split(land_b[c])
        out[0] += dot3(h, l, one_h[cols(c), :], one_l[cols(c), :])

    @pl.when(jnp.logical_not(even))
    def _():
        pl.semaphore_wait(barrier, jnp.where(is_rel, 6, 4))

        def left_factor():
            def body(c, _):
                row(c).wait_recv()
                fill_lhs(c, 0)
                return 0

            lax.fori_loop(0, nch, body, 0)

        def product(c, _):
            stage_a[c] = dot3(
                lhs_h[0:rows, :], lhs_l[0:rows, :], one_h[:, cols(c)], one_l[:, cols(c)]
            )
            xo(c).start()
            return 0

        lag = 5

        def process(c):
            to_sib(c).start()
            hi, lo = split(full[c])
            one_h[:, cols(c)] = hi
            one_l[:, cols(c)] = lo

            @pl.when(c == lag)
            def _():
                left_factor()
                lax.fori_loop(0, lag, product, 0)

            @pl.when(c >= lag)
            def _():
                product(c, 0)

        gather(process, rest_of_block)
        out[...] = jnp.zeros_like(out)

        def body(c, _):
            @pl.when(c == mine)
            def _():
                hand_on((1, 2))

            send_b(c).wait_recv()
            add_chunk(c)
            return 0

        lax.fori_loop(0, nch, body, 0)

        def finish(c, _):
            row(c).wait_send()
            to_sib(c).wait_send()
            xo(c).wait_send()
            return 0

        lax.fori_loop(0, nch, finish, 0)
        lax.fori_loop(0, nch, drain, 0)

        handed((1, 2))
    @pl.when(even)
    def _():
        pl.semaphore_wait(barrier, jnp.where(is_src, 5 + sum(n_rel), jnp.where(is_rel, 7, 5)))
        rest_of_block()

        hand_on((0,))

        def fill(c, _):
            row(c).wait_recv()
            fill_lhs(c, 0)
            return 0

        lax.fori_loop(0, nch, fill, 0)

        def take(c, _):
            to_sib(c).wait_recv()
            hi, lo = split(sib[c])
            one_h[:, cols(c)] = hi
            one_l[:, cols(c)] = lo
            return 0

        lax.fori_loop(0, START, take, 0)
        def process(c):
            @pl.when(c == 0)
            def _():
                lax.fori_loop(START, nch, take, 0)

                def body(k, _):
                    xo(k).wait_recv()
                    hi, lo = split(land_a[k])
                    lhs_h[rows : 2 * rows, cols(k)] = hi
                    lhs_l[rows : 2 * rows, cols(k)] = lo
                    return 0

                lax.fori_loop(0, nch, body, 0)

            bh, bl = split(full[c])
            own_h[:, cols(c)] = bh
            own_l[:, cols(c)] = bl
            stage_a[c] = dot3(lhs_h[0:rows, :], lhs_l[0:rows, :], bh, bl)
            start(1, c)
            stage_b[c] = dot3(lhs_h[rows:, :], lhs_l[rows:, :], bh, bl)
            start(2, c)

        gather(process, lambda: None)

        def collect(c, _):
            send_a(c).wait_recv()
            hi, lo = split(land_b[c])
            lhs_h[0:rows, cols(c)] = hi
            lhs_l[0:rows, cols(c)] = lo
            return 0

        lax.fori_loop(0, nch - FOLD, collect, 0)

        cut = (nch - FOLD) * WIDE
        wide = 2 * WIDE
        parts = [slice(k * wide, (k + 1) * wide) for k in range(nch // 2)]
        fh, fl = lhs_h[0:rows, 0:cut], lhs_l[0:rows, 0:cut]
        for part in parts:
            x = dot3(fh, fl, one_h[0:cut, part], one_l[0:cut, part])
            lhs_h[rows:, part], lhs_l[rows:, part] = split(x)
        xh, xl = lhs_h[rows:, :], lhs_l[rows:, :]
        gh, gl = one_h[cut:, :], one_l[cut:, :]
        for part in parts:
            vh, vl = own_h[:, part], own_l[:, part]
            out[0, :, part] = dot3(xh, xl, vh, vl)
            meet_h[:, part], meet_l[:, part] = split(dot3(gh, gl, vh, vl))

        lax.fori_loop(nch - FOLD, nch, collect, 0)
        lh, ll = lhs_h[0:rows, cut:], lhs_l[0:rows, cut:]
        for part in parts:
            out[0, :, part] += dot3(lh, ll, meet_h[:, part], meet_l[:, part])

        def finish(c, _):
            @pl.when(jnp.logical_not(is_src))
            def _():
                row(c).wait_send()

            send_a(c).wait_send()
            send_b(c).wait_send()
            return 0

        lax.fori_loop(0, nch, finish, 0)
        lax.fori_loop(0, nch, drain, 0)

        handed((0,))


def per_device(n_t, n_r, coupling, field):
    _, rows, sites = coupling.shape
    nch = sites // WIDE
    dma = pltpu.SemaphoreType.DMA
    piece = pltpu.VMEM((nch, rows, WIDE), F32)
    whole = pltpu.VMEM((nch, sites, WIDE), F32)
    done = pl.pallas_call(
        functools.partial(kernel, n_t, n_r),
        out_shape=jax.ShapeDtypeStruct((1, rows, sites), F32),
        in_specs=[
            pl.BlockSpec(memory_space=pltpu.VMEM),
            pl.BlockSpec(memory_space=pltpu.VMEM),
        ],
        out_specs=pl.BlockSpec(memory_space=pltpu.VMEM),
        scratch_shapes=[
            whole,
            whole,
            piece,
            pltpu.VMEM((2 * rows, sites), BF16),
            pltpu.VMEM((2 * rows, sites), BF16),
            pltpu.VMEM((sites, sites), BF16),
            pltpu.VMEM((sites, sites), BF16),
            pltpu.VMEM((sites, sites), BF16),
            pltpu.VMEM((sites, sites), BF16),
            piece,
            piece,
            piece,
            piece,
            pltpu.VMEM((FOLD * WIDE, sites), BF16),
            pltpu.VMEM((FOLD * WIDE, sites), BF16),
            pltpu.VMEM((2, rows, WIDE), F32),
            pltpu.SemaphoreType.REGULAR,
            dma((2,)),
            dma((2,)),
            dma((2, nch)),
            dma((2, nch)),
            dma((2, nch)),
            dma((2, nch)),
            dma((nch,)),
            dma((nch,)),
            dma((nch,)),
            dma((nch,)),
            dma((nch,)),
            dma((nch,)),
            dma((nch,)),
            dma((nch,)),
            dma((nch,)),
            dma((nch,)),
        ],
        compiler_params=pltpu.CompilerParams(
            collective_id=0, has_side_effects=True, vmem_limit_bytes=40 * 2**20
        ),
        cost_estimate=pl.CostEstimate(
            flops=18 * rows * sites * sites, bytes_accessed=8 * rows * sites, transcendentals=0
        ),
    )(coupling, field)
    pieces = 4

    def write(src, dst, sems):
        step = rows // pieces
        copies = [
            pltpu.make_async_copy(
                src.at[0, pl.ds(i * step, step)], dst.at[0, pl.ds(i * step, step)], sems.at[i]
            )
            for i in range(pieces)
        ]
        for c in copies:
            c.start()
        for c in copies:
            c.wait()

    return pl.pallas_call(
        write,
        out_shape=jax.ShapeDtypeStruct((1, rows, sites), F32),
        in_specs=[pl.BlockSpec(memory_space=pl.ANY)],
        out_specs=pl.BlockSpec(memory_space=pl.ANY),
        scratch_shapes=[dma((pieces,))],
        compiler_params=pltpu.CompilerParams(vmem_limit_bytes=2**20),
    )(done)


def solution(mesh):
    return jax.shard_map(
        functools.partial(per_device, mesh.shape["tm"], mesh.shape["rows"]),
        mesh=mesh,
        in_specs=(P("tm", "rows", None), P("tm", "rows")),
        out_specs=P("tm", "rows", None),
        check_vma=False,
    )
```

```python
import functools

import jax
import jax.numpy as jnp
from jax import lax
from jax.experimental import pallas as pl
from jax.experimental.pallas import tpu as pltpu
from jax.sharding import PartitionSpec as P

F32 = jnp.float32
BF16 = jnp.bfloat16
MESH = pl.DeviceIdType.MESH

WIDE = 128
AHEAD = 2
FOLD = 2
LEAD = 1
START = 5


def split(x):
    hi = x.astype(BF16)
    return hi, (x - hi.astype(F32)).astype(BF16)


def dot3(ah, al, bh, bl):
    def mm(a, b):
        return jnp.dot(a, b, preferred_element_type=F32)

    return mm(ah, bh) + (mm(ah, bl) + mm(al, bh))


def kernel(
    n_t, n_r, coupling, field, out,
    raw, levels, full, sib, rowbuf, lhs_h, lhs_l, own_h, own_l, one_h, one_l,
    stage_a, stage_b, land_a, land_b, meet_h, meet_l,
    rel, load_sem, pace, rel_s, rel_r,
    own_s, own_r, fwd_s, fwd_r, sib_s, sib_r, xo_s, xo_r, row_s, row_r, a_s, a_r, b_s, b_r,
):
    t = lax.axis_index("tm")
    r = lax.axis_index("rows")
    rows = coupling.shape[1]
    nch = full.shape[0]
    even = lax.rem(t, 2) == 0
    half = rows // 2
    span = n_t // 2
    place = lax.rem(t, span)
    base = t - place
    other = span - base
    line = 16
    n_rel = (nch, nch - 1, nch - 1)
    odd = jnp.logical_not(even)
    is_src = place == 0
    is_dst = place >= span - 2
    kind = place // line - 1
    mine = lax.rem(place, line) // 2
    is_rel = jnp.logical_or(
        jnp.logical_and(even, kind == 0),
        jnp.logical_and(odd, jnp.logical_and(kind > 0, mine < n_rel[1])),
    )

    def way(k, c):
        return (k + 1) * line + 2 * c + (1 if k else 0)

    def tm(by):
        return lax.rem(t + by + n_t, n_t)

    def at_t(by):
        return (tm(by), r)

    def at_r(by):
        return (t, lax.rem(r + by + n_r, n_r))

    def plane(by):
        return pl.multiple_of(lax.rem(r + by + n_r, n_r) * rows, rows)

    def cols(c):
        return pl.ds(pl.multiple_of(c * WIDE, WIDE), WIDE)

    def load(c):
        src = coupling.at[0, :, cols(c)]
        return pltpu.make_async_copy(src, raw.at[:, cols(c)], load_sem.at[c])

    load_levels = pltpu.make_async_copy(field, levels, load_sem.at[nch])
    load_levels.start()
    for c in range(nch):
        load(c).start()

    barrier = pltpu.get_barrier_semaphore()
    for by in (1, -1):
        pl.semaphore_signal(barrier, inc=1, device_id=at_r(by), device_id_type=MESH)
    pl.semaphore_signal(barrier, inc=1, device_id=at_t(1), device_id_type=MESH)

    @pl.when(even)
    def _():
        pl.semaphore_signal(barrier, inc=1, device_id=at_t(2), device_id_type=MESH)

    @pl.when(is_rel)
    def _():
        for to in (base, other + place):
            pl.semaphore_signal(barrier, inc=1, device_id=(to, r), device_id_type=MESH)

    beside = (other + place, r)
    pl.semaphore_signal(barrier, inc=1, device_id=beside, device_id_type=MESH)

    def greet(k):
        for c in range(n_rel[k]):
            to = (base + way(k, c), r)
            pl.semaphore_signal(barrier, inc=1, device_id=to, device_id_type=MESH)

    @pl.when(jnp.logical_and(is_dst, even))
    def _():
        greet(1)

    @pl.when(jnp.logical_and(is_dst, odd))
    def _():
        greet(0)
        greet(2)

    def copy(src, dst, ssem, rsem, dev):
        return pltpu.make_async_remote_copy(
            src_ref=src, dst_ref=dst, send_sem=ssem, recv_sem=rsem,
            device_id=dev, device_id_type=MESH,
        )

    def own(c, d):
        piece = full.at[c, pl.ds(plane(0), rows), :]
        return copy(piece, piece, own_s.at[d, c], own_r.at[d, c], at_r(1 - 2 * d))

    def own_in(c, d):
        piece = full.at[c, pl.ds(plane(2 * d - 1), rows), :]
        return copy(piece, piece, own_s.at[d, c], own_r.at[d, c], at_r(1 - 2 * d))

    def fwd(c, d):
        piece = full.at[c, pl.ds(pl.multiple_of(plane(2 * d - 1) + d * half, half), half), :]
        return copy(piece, piece, fwd_s.at[d, c], fwd_r.at[d, c], at_r(1 - 2 * d))

    def fwd_in(c, d):
        piece = full.at[c, pl.ds(pl.multiple_of(plane(2) + d * half, half), half), :]
        return copy(piece, piece, fwd_s.at[d, c], fwd_r.at[d, c], at_r(1 - 2 * d))

    def to_sib(c):
        return copy(full.at[c], sib.at[c], sib_s.at[c], sib_r.at[c], at_t(-1))

    def xo(c):
        return copy(stage_a.at[c], land_a.at[c], xo_s.at[c], xo_r.at[c], at_t(-1))

    def row(c):
        piece = full.at[c, pl.ds(plane(0), rows), :]
        return copy(piece, rowbuf.at[c], row_s.at[c], row_r.at[c], at_t(-1))

    def send_a(c):
        return copy(stage_a.at[c], land_b.at[c], a_s.at[c], a_r.at[c], at_t(-2))

    def send_b(c):
        return copy(stage_b.at[c], land_b.at[c], b_s.at[c], b_r.at[c], at_t(-1))

    def by_way(k, c):
        src = (full.at[c, pl.ds(plane(0), rows), :], stage_a.at[c], stage_b.at[c])[k]
        sem = (row_s, a_s, b_s)[k].at[c]
        return copy(src, rel.at[0], sem, rel_r.at[0], (base + way(k, c), r))

    def start(k, c):
        go = (row, send_a, send_b)[k]
        by = jnp.logical_and(is_src, c < n_rel[k])

        @pl.when(by)
        def _():
            by_way(k, c).start()

        @pl.when(jnp.logical_not(by))
        def _():
            go(c).start()

    def over():
        return copy(rel.at[0], rel.at[1], rel_s.at[0], rel_r.at[1], (other + place, r))

    def last_leg(k):
        dst, sem, back = ((rowbuf, row_r, 1), (land_b, a_r, 2), (land_b, b_r, 1))[k]
        to = (lax.rem(other - back + n_t, n_t), r)
        return copy(rel.at[1], dst.at[mine], rel_s.at[1], sem.at[mine], to)

    def hand_on(kinds):
        @pl.when(is_rel)
        def _():
            copy(rel.at[0], rel.at[0], rel_s.at[0], rel_r.at[0], (base, r)).wait_recv()
            over().start()
            over().wait_recv()

        for k in kinds:

            @pl.when(jnp.logical_and(is_rel, kind == k))
            def _():
                last_leg(k).start()

    def handed(kinds):
        for k in kinds:

            @pl.when(jnp.logical_and(is_rel, kind == k))
            def _():
                over().wait_send()
                last_leg(k).wait_send()

    load_levels.wait()
    scale = jnp.exp(jnp.transpose(jnp.broadcast_to(levels[...], (WIDE, rows))))
    row_ids = lax.broadcasted_iota(jnp.int32, (rows, WIDE), 0) + r * rows
    col_ids = lax.broadcasted_iota(jnp.int32, (rows, WIDE), 1)

    def build(c, _):
        load(c).wait()
        ident = jnp.where(row_ids == col_ids + c * WIDE, 1.0, 0.0).astype(F32)
        full[c, pl.ds(plane(0), rows), :] = scale * (ident + raw[:, cols(c)])
        return 0

    lax.fori_loop(0, AHEAD, build, 0)

    def rest_of_block():
        lax.fori_loop(AHEAD, nch, build, 0)

        def send(c, _):
            start(0, c)

            @pl.when(is_src)
            def _():
                row(c).wait_send()

            return 0

        lax.fori_loop(0, nch, send, 0)

    def gather(process, before):
        for c in range(AHEAD):
            for d in (0, 1):
                own(c, d).start()
        before()

        def step(c, _):
            @pl.when(c < nch)
            def _():
                for d in (0, 1):
                    own_in(c, d).wait_recv()
                    fwd(c, d).start()

            @pl.when(c + AHEAD + LEAD < nch)
            def _():
                pl.semaphore_signal(pace, inc=1, device_id=beside, device_id_type=MESH)

            @pl.when(c + AHEAD < nch)
            def _():
                @pl.when(c >= LEAD)
                def _():
                    pl.semaphore_wait(pace, 1)

                for d in (0, 1):
                    own(c + AHEAD, d).start()

            @pl.when(c >= 1)
            def _():
                for d in (0, 1):
                    fwd_in(c - 1, d).wait_recv()
                process(c - 1)

            return 0

        lax.fori_loop(0, nch + 1, step, 0)

    def drain(c, _):
        for d in (0, 1):
            own(c, d).wait_send()
            fwd(c, d).wait_send()
        return 0

    def fill_lhs(c, first):
        hi, lo = split(rowbuf[c])
        lhs_h[first : first + rows, cols(c)] = hi
        lhs_l[first : first + rows, cols(c)] = lo

    def add_chunk(c):
        h, l = split(land_b[c])
        out[0] += dot3(h, l, one_h[cols(c), :], one_l[cols(c), :])

    @pl.when(jnp.logical_not(even))
    def _():
        pl.semaphore_wait(barrier, jnp.where(is_rel, 6, 4))

        def left_factor():
            def body(c, _):
                row(c).wait_recv()
                fill_lhs(c, 0)
                return 0

            lax.fori_loop(0, nch, body, 0)

        def product(c, _):
            stage_a[c] = dot3(
                lhs_h[0:rows, :], lhs_l[0:rows, :], one_h[:, cols(c)], one_l[:, cols(c)]
            )
            xo(c).start()
            return 0

        lag = 5

        def process(c):
            to_sib(c).start()
            hi, lo = split(full[c])
            one_h[:, cols(c)] = hi
            one_l[:, cols(c)] = lo

            @pl.when(c == lag)
            def _():
                left_factor()
                lax.fori_loop(0, lag, product, 0)

            @pl.when(c >= lag)
            def _():
                product(c, 0)

        gather(process, rest_of_block)
        out[...] = jnp.zeros_like(out)

        def body(c, _):
            @pl.when(c == mine)
            def _():
                hand_on((1, 2))

            send_b(c).wait_recv()
            add_chunk(c)
            return 0

        lax.fori_loop(0, nch, body, 0)

        def finish(c, _):
            row(c).wait_send()
            to_sib(c).wait_send()
            xo(c).wait_send()
            return 0

        lax.fori_loop(0, nch, finish, 0)
        lax.fori_loop(0, nch, drain, 0)

        handed((1, 2))
    @pl.when(even)
    def _():
        pl.semaphore_wait(barrier, jnp.where(is_src, 5 + sum(n_rel), jnp.where(is_rel, 7, 5)))
        rest_of_block()

        hand_on((0,))

        def fill(c, _):
            row(c).wait_recv()
            fill_lhs(c, 0)
            return 0

        lax.fori_loop(0, nch, fill, 0)

        def take(c, _):
            to_sib(c).wait_recv()
            hi, lo = split(sib[c])
            one_h[:, cols(c)] = hi
            one_l[:, cols(c)] = lo
            return 0

        lax.fori_loop(0, START, take, 0)
        def process(c):
            @pl.when(c == 0)
            def _():
                lax.fori_loop(START, nch, take, 0)

                def body(k, _):
                    xo(k).wait_recv()
                    hi, lo = split(land_a[k])
                    lhs_h[rows : 2 * rows, cols(k)] = hi
                    lhs_l[rows : 2 * rows, cols(k)] = lo
                    return 0

                lax.fori_loop(0, nch, body, 0)

            bh, bl = split(full[c])
            own_h[:, cols(c)] = bh
            own_l[:, cols(c)] = bl
            stage_a[c] = dot3(lhs_h[0:rows, :], lhs_l[0:rows, :], bh, bl)
            start(1, c)
            stage_b[c] = dot3(lhs_h[rows:, :], lhs_l[rows:, :], bh, bl)
            start(2, c)

        gather(process, lambda: None)

        def collect(c, _):
            send_a(c).wait_recv()
            hi, lo = split(land_b[c])
            lhs_h[0:rows, cols(c)] = hi
            lhs_l[0:rows, cols(c)] = lo
            return 0

        lax.fori_loop(0, nch - FOLD, collect, 0)

        cut = (nch - FOLD) * WIDE
        wide = 2 * WIDE
        parts = [slice(k * wide, (k + 1) * wide) for k in range(nch // 2)]
        fh, fl = lhs_h[0:rows, 0:cut], lhs_l[0:rows, 0:cut]
        for part in parts:
            x = dot3(fh, fl, one_h[0:cut, part], one_l[0:cut, part])
            lhs_h[rows:, part], lhs_l[rows:, part] = split(x)
        xh, xl = lhs_h[rows:, :], lhs_l[rows:, :]
        gh, gl = one_h[cut:, :], one_l[cut:, :]
        for part in parts:
            vh, vl = own_h[:, part], own_l[:, part]
            out[0, :, part] = dot3(xh, xl, vh, vl)
            meet_h[:, part], meet_l[:, part] = split(dot3(gh, gl, vh, vl))

        lax.fori_loop(nch - FOLD, nch, collect, 0)
        lh, ll = lhs_h[0:rows, cut:], lhs_l[0:rows, cut:]
        for part in parts:
            out[0, :, part] += dot3(lh, ll, meet_h[:, part], meet_l[:, part])

        def finish(c, _):
            @pl.when(jnp.logical_not(is_src))
            def _():
                row(c).wait_send()

            send_a(c).wait_send()
            send_b(c).wait_send()
            return 0

        lax.fori_loop(0, nch, finish, 0)
        lax.fori_loop(0, nch, drain, 0)

        handed((0,))


def per_device(n_t, n_r, coupling, field):
    _, rows, sites = coupling.shape
    nch = sites // WIDE
    dma = pltpu.SemaphoreType.DMA
    piece = pltpu.VMEM((nch, rows, WIDE), F32)
    whole = pltpu.VMEM((nch, sites, WIDE), F32)
    done = pl.pallas_call(
        functools.partial(kernel, n_t, n_r),
        out_shape=jax.ShapeDtypeStruct((1, rows, sites), F32),
        in_specs=[
            pl.BlockSpec(memory_space=pltpu.HBM),
            pl.BlockSpec(memory_space=pltpu.HBM),
        ],
        out_specs=pl.BlockSpec(memory_space=pltpu.VMEM),
        scratch_shapes=[
            pltpu.VMEM((rows, sites), F32),
            pltpu.VMEM((1, rows), F32),
            whole,
            whole,
            piece,
            pltpu.VMEM((2 * rows, sites), BF16),
            pltpu.VMEM((2 * rows, sites), BF16),
            pltpu.VMEM((sites, sites), BF16),
            pltpu.VMEM((sites, sites), BF16),
            pltpu.VMEM((sites, sites), BF16),
            pltpu.VMEM((sites, sites), BF16),
            piece,
            piece,
            piece,
            piece,
            pltpu.VMEM((FOLD * WIDE, sites), BF16),
            pltpu.VMEM((FOLD * WIDE, sites), BF16),
            pltpu.VMEM((2, rows, WIDE), F32),
            dma((nch + 1,)),
            pltpu.SemaphoreType.REGULAR,
            dma((2,)),
            dma((2,)),
            dma((2, nch)),
            dma((2, nch)),
            dma((2, nch)),
            dma((2, nch)),
            dma((nch,)),
            dma((nch,)),
            dma((nch,)),
            dma((nch,)),
            dma((nch,)),
            dma((nch,)),
            dma((nch,)),
            dma((nch,)),
            dma((nch,)),
            dma((nch,)),
        ],
        compiler_params=pltpu.CompilerParams(
            collective_id=0, has_side_effects=True, vmem_limit_bytes=52 * 2**20
        ),
        cost_estimate=pl.CostEstimate(
            flops=18 * rows * sites * sites, bytes_accessed=8 * rows * sites, transcendentals=0
        ),
    )(coupling, field)
    pieces = 4

    def write(src, dst, sems):
        step = rows // pieces
        copies = [
            pltpu.make_async_copy(
                src.at[0, pl.ds(i * step, step)], dst.at[0, pl.ds(i * step, step)], sems.at[i]
            )
            for i in range(pieces)
        ]
        for c in copies:
            c.start()
        for c in copies:
            c.wait()

    return pl.pallas_call(
        write,
        out_shape=jax.ShapeDtypeStruct((1, rows, sites), F32),
        in_specs=[pl.BlockSpec(memory_space=pl.ANY)],
        out_specs=pl.BlockSpec(memory_space=pl.ANY),
        scratch_shapes=[dma((pieces,))],
        compiler_params=pltpu.CompilerParams(vmem_limit_bytes=2**20),
    )(done)


def solution(mesh):
    return jax.shard_map(
        functools.partial(per_device, mesh.shape["tm"], mesh.shape["rows"]),
        mesh=mesh,
        in_specs=(P("tm", "rows", None), P("tm", "rows")),
        out_specs=P("tm", "rows", None),
        check_vma=False,
    )
```

```python
import functools

import jax
import jax.numpy as jnp
from jax import lax
from jax.experimental import pallas as pl
from jax.experimental.pallas import tpu as pltpu
from jax.sharding import PartitionSpec as P

F32 = jnp.float32
BF16 = jnp.bfloat16
MESH = pl.DeviceIdType.MESH

WIDE = 128
AHEAD = 2
FOLD = 2
LEAD = 1
HOLD = 1
START = 5


def split(x):
    hi = x.astype(BF16)
    return hi, (x - hi.astype(F32)).astype(BF16)


def dot3(ah, al, bh, bl):
    def mm(a, b):
        return jnp.dot(a, b, preferred_element_type=F32)

    return mm(ah, bh) + (mm(ah, bl) + mm(al, bh))


def kernel(
    n_t, n_r, coupling, field, out,
    raw, levels, full, sib, rowbuf, lhs_h, lhs_l, own_h, own_l, one_h, one_l,
    stage_a, stage_b, land_a, land_b, meet_h, meet_l,
    rel, load_sem, pace, rel_s, rel_r,
    own_s, own_r, fwd_s, fwd_r, sib_s, sib_r, xo_s, xo_r, row_s, row_r, a_s, a_r, b_s, b_r,
):
    t = lax.axis_index("tm")
    r = lax.axis_index("rows")
    rows = coupling.shape[1]
    nch = full.shape[0]
    even = lax.rem(t, 2) == 0
    half = rows // 2
    span = n_t // 2
    place = lax.rem(t, span)
    base = t - place
    other = span - base
    line = 16
    n_rel = (nch, nch - 1, nch - 1)
    odd = jnp.logical_not(even)
    is_src = place == 0
    is_dst = place >= span - 2
    kind = place // line - 1
    mine = lax.rem(place, line) // 2
    is_rel = jnp.logical_or(
        jnp.logical_and(even, kind == 0),
        jnp.logical_and(odd, jnp.logical_and(kind > 0, mine < n_rel[1])),
    )

    def way(k, c):
        return (k + 1) * line + 2 * c + (1 if k else 0)

    def tm(by):
        return lax.rem(t + by + n_t, n_t)

    def at_t(by):
        return (tm(by), r)

    def at_r(by):
        return (t, lax.rem(r + by + n_r, n_r))

    def plane(by):
        return pl.multiple_of(lax.rem(r + by + n_r, n_r) * rows, rows)

    def cols(c):
        return pl.ds(pl.multiple_of(c * WIDE, WIDE), WIDE)

    def load(c):
        src = coupling.at[0, :, cols(c)]
        return pltpu.make_async_copy(src, raw.at[:, cols(c)], load_sem.at[c])

    load_levels = pltpu.make_async_copy(field, levels, load_sem.at[nch])
    load_levels.start()
    for c in range(nch):
        load(c).start()

    barrier = pltpu.get_barrier_semaphore()
    for by in (1, -1):
        pl.semaphore_signal(barrier, inc=1, device_id=at_r(by), device_id_type=MESH)
    pl.semaphore_signal(barrier, inc=1, device_id=at_t(1), device_id_type=MESH)

    @pl.when(even)
    def _():
        pl.semaphore_signal(barrier, inc=1, device_id=at_t(2), device_id_type=MESH)

    @pl.when(is_rel)
    def _():
        for to in (base, other + place):
            pl.semaphore_signal(barrier, inc=1, device_id=(to, r), device_id_type=MESH)

    beside = (other + place, r)
    pl.semaphore_signal(barrier, inc=1, device_id=beside, device_id_type=MESH)

    def greet(k):
        for c in range(n_rel[k]):
            to = (base + way(k, c), r)
            pl.semaphore_signal(barrier, inc=1, device_id=to, device_id_type=MESH)

    @pl.when(jnp.logical_and(is_dst, even))
    def _():
        greet(1)

    @pl.when(jnp.logical_and(is_dst, odd))
    def _():
        greet(0)
        greet(2)

    def copy(src, dst, ssem, rsem, dev):
        return pltpu.make_async_remote_copy(
            src_ref=src, dst_ref=dst, send_sem=ssem, recv_sem=rsem,
            device_id=dev, device_id_type=MESH,
        )

    def own(c, d):
        piece = full.at[c, pl.ds(plane(0), rows), :]
        return copy(piece, piece, own_s.at[d, c], own_r.at[d, c], at_r(1 - 2 * d))

    def own_in(c, d):
        piece = full.at[c, pl.ds(plane(2 * d - 1), rows), :]
        return copy(piece, piece, own_s.at[d, c], own_r.at[d, c], at_r(1 - 2 * d))

    def fwd(c, d):
        piece = full.at[c, pl.ds(pl.multiple_of(plane(2 * d - 1) + d * half, half), half), :]
        return copy(piece, piece, fwd_s.at[d, c], fwd_r.at[d, c], at_r(1 - 2 * d))

    def fwd_in(c, d):
        piece = full.at[c, pl.ds(pl.multiple_of(plane(2) + d * half, half), half), :]
        return copy(piece, piece, fwd_s.at[d, c], fwd_r.at[d, c], at_r(1 - 2 * d))

    def to_sib(c):
        return copy(full.at[c], sib.at[c], sib_s.at[c], sib_r.at[c], at_t(-1))

    def xo(c):
        return copy(stage_a.at[c], land_a.at[c], xo_s.at[c], xo_r.at[c], at_t(-1))

    def row(c):
        piece = full.at[c, pl.ds(plane(0), rows), :]
        return copy(piece, rowbuf.at[c], row_s.at[c], row_r.at[c], at_t(-1))

    def send_a(c):
        return copy(stage_a.at[c], land_b.at[c], a_s.at[c], a_r.at[c], at_t(-2))

    def send_b(c):
        return copy(stage_b.at[c], land_b.at[c], b_s.at[c], b_r.at[c], at_t(-1))

    def by_way(k, c):
        src = (full.at[c, pl.ds(plane(0), rows), :], stage_a.at[c], stage_b.at[c])[k]
        sem = (row_s, a_s, b_s)[k].at[c]
        return copy(src, rel.at[0], sem, rel_r.at[0], (base + way(k, c), r))

    def start(k, c):
        go = (row, send_a, send_b)[k]
        by = jnp.logical_and(is_src, c < n_rel[k])

        @pl.when(by)
        def _():
            by_way(k, c).start()

        @pl.when(jnp.logical_not(by))
        def _():
            go(c).start()

    def over():
        return copy(rel.at[0], rel.at[1], rel_s.at[0], rel_r.at[1], (other + place, r))

    def last_leg(k):
        dst, sem, back = ((rowbuf, row_r, 1), (land_b, a_r, 2), (land_b, b_r, 1))[k]
        to = (lax.rem(other - back + n_t, n_t), r)
        return copy(rel.at[1], dst.at[mine], rel_s.at[1], sem.at[mine], to)

    def hand_on(kinds):
        @pl.when(is_rel)
        def _():
            copy(rel.at[0], rel.at[0], rel_s.at[0], rel_r.at[0], (base, r)).wait_recv()
            over().start()
            over().wait_recv()

        for k in kinds:

            @pl.when(jnp.logical_and(is_rel, kind == k))
            def _():
                last_leg(k).start()

    def handed(kinds):
        for k in kinds:

            @pl.when(jnp.logical_and(is_rel, kind == k))
            def _():
                over().wait_send()
                last_leg(k).wait_send()

    load_levels.wait()
    scale = jnp.exp(jnp.transpose(jnp.broadcast_to(levels[...], (WIDE, rows))))
    row_ids = lax.broadcasted_iota(jnp.int32, (rows, WIDE), 0) + r * rows
    col_ids = lax.broadcasted_iota(jnp.int32, (rows, WIDE), 1)

    def build(c, _):
        load(c).wait()
        ident = jnp.where(row_ids == col_ids + c * WIDE, 1.0, 0.0).astype(F32)
        full[c, pl.ds(plane(0), rows), :] = scale * (ident + raw[:, cols(c)])
        return 0

    lax.fori_loop(0, AHEAD, build, 0)

    def rest_of_block():
        lax.fori_loop(AHEAD, nch, build, 0)

        def send(c, _):
            start(0, c)

            @pl.when(is_src)
            def _():
                row(c).wait_send()

            return 0

        lax.fori_loop(0, nch, send, 0)

    def gather(process, before, done):
        for c in range(AHEAD):
            for d in (0, 1):
                own(c, d).start()
        before()

        def step(c, _):
            @pl.when(c < nch)
            def _():
                for d in (0, 1):
                    own_in(c, d).wait_recv()
                    fwd(c, d).start()

            @pl.when(c + AHEAD + LEAD < nch)
            def _():
                pl.semaphore_signal(pace, inc=1, device_id=beside, device_id_type=MESH)

            @pl.when(c + AHEAD < nch)
            def _():
                @pl.when(c >= LEAD)
                def _():
                    pl.semaphore_wait(pace, 1)

                for d in (0, 1):
                    own(c + AHEAD, d).start()

            def take_in(k, _):
                for d in (0, 1):
                    fwd_in(k, d).wait_recv()
                process(k)
                return 0

            lax.fori_loop(done(c - 1), done(c), take_in, 0)
            return 0

        lax.fori_loop(0, nch + 1, step, 0)

    def drain(c, _):
        for d in (0, 1):
            own(c, d).wait_send()
            fwd(c, d).wait_send()
        return 0

    def fill_lhs(c, first):
        hi, lo = split(rowbuf[c])
        lhs_h[first : first + rows, cols(c)] = hi
        lhs_l[first : first + rows, cols(c)] = lo

    def add_chunk(c):
        h, l = split(land_b[c])
        out[0] += dot3(h, l, one_h[cols(c), :], one_l[cols(c), :])

    @pl.when(jnp.logical_not(even))
    def _():
        pl.semaphore_wait(barrier, jnp.where(is_rel, 6, 4))

        def left_factor():
            def body(c, _):
                row(c).wait_recv()
                fill_lhs(c, 0)
                return 0

            lax.fori_loop(0, nch, body, 0)

        def product(c, _):
            stage_a[c] = dot3(
                lhs_h[0:rows, :], lhs_l[0:rows, :], one_h[:, cols(c)], one_l[:, cols(c)]
            )
            xo(c).start()
            return 0

        lag = 5

        def process(c):
            to_sib(c).start()
            hi, lo = split(full[c])
            one_h[:, cols(c)] = hi
            one_l[:, cols(c)] = lo

            @pl.when(c == lag)
            def _():
                left_factor()
                lax.fori_loop(0, lag, product, 0)

            @pl.when(c >= lag)
            def _():
                product(c, 0)

        gather(process, rest_of_block, lambda c: jnp.maximum(c, 0))
        out[...] = jnp.zeros_like(out)

        def body(c, _):
            @pl.when(c == mine)
            def _():
                hand_on((1, 2))

            send_b(c).wait_recv()
            add_chunk(c)
            return 0

        lax.fori_loop(0, nch, body, 0)

        def finish(c, _):
            row(c).wait_send()
            to_sib(c).wait_send()
            xo(c).wait_send()
            return 0

        lax.fori_loop(0, nch, finish, 0)
        lax.fori_loop(0, nch, drain, 0)

        handed((1, 2))
    @pl.when(even)
    def _():
        pl.semaphore_wait(barrier, jnp.where(is_src, 5 + sum(n_rel), jnp.where(is_rel, 7, 5)))
        rest_of_block()

        hand_on((0,))

        def fill(c, _):
            row(c).wait_recv()
            fill_lhs(c, 0)
            return 0

        lax.fori_loop(0, nch, fill, 0)

        def take(c, _):
            to_sib(c).wait_recv()
            hi, lo = split(sib[c])
            one_h[:, cols(c)] = hi
            one_l[:, cols(c)] = lo
            return 0

        lax.fori_loop(0, START, take, 0)
        def process(c):
            @pl.when(c == 0)
            def _():
                lax.fori_loop(START, nch, take, 0)

                def body(k, _):
                    xo(k).wait_recv()
                    hi, lo = split(land_a[k])
                    lhs_h[rows : 2 * rows, cols(k)] = hi
                    lhs_l[rows : 2 * rows, cols(k)] = lo
                    return 0

                lax.fori_loop(0, nch, body, 0)

            bh, bl = split(full[c])
            stage_a[c] = dot3(lhs_h[0:rows, :], lhs_l[0:rows, :], bh, bl)
            start(1, c)
            stage_b[c] = dot3(lhs_h[rows:, :], lhs_l[rows:, :], bh, bl)
            start(2, c)
            own_h[:, cols(c)] = bh
            own_l[:, cols(c)] = bl

        def done(c):
            return jnp.maximum(jnp.minimum(2 * (c - HOLD), c), 0)

        gather(process, lambda: None, done)

        def collect(c, _):
            send_a(c).wait_recv()
            hi, lo = split(land_b[c])
            lhs_h[0:rows, cols(c)] = hi
            lhs_l[0:rows, cols(c)] = lo
            return 0

        lax.fori_loop(0, nch - FOLD, collect, 0)

        cut = (nch - FOLD) * WIDE
        wide = 2 * WIDE
        parts = [slice(k * wide, (k + 1) * wide) for k in range(nch // 2)]
        fh, fl = lhs_h[0:rows, 0:cut], lhs_l[0:rows, 0:cut]
        for part in parts:
            x = dot3(fh, fl, one_h[0:cut, part], one_l[0:cut, part])
            lhs_h[rows:, part], lhs_l[rows:, part] = split(x)
        xh, xl = lhs_h[rows:, :], lhs_l[rows:, :]
        gh, gl = one_h[cut:, :], one_l[cut:, :]
        for part in parts:
            vh, vl = own_h[:, part], own_l[:, part]
            out[0, :, part] = dot3(xh, xl, vh, vl)
            meet_h[:, part], meet_l[:, part] = split(dot3(gh, gl, vh, vl))

        lax.fori_loop(nch - FOLD, nch, collect, 0)
        lh, ll = lhs_h[0:rows, cut:], lhs_l[0:rows, cut:]
        for part in parts:
            out[0, :, part] += dot3(lh, ll, meet_h[:, part], meet_l[:, part])

        def finish(c, _):
            @pl.when(jnp.logical_not(is_src))
            def _():
                row(c).wait_send()

            send_a(c).wait_send()
            send_b(c).wait_send()
            return 0

        lax.fori_loop(0, nch, finish, 0)
        lax.fori_loop(0, nch, drain, 0)

        handed((0,))


def per_device(n_t, n_r, coupling, field):
    _, rows, sites = coupling.shape
    nch = sites // WIDE
    dma = pltpu.SemaphoreType.DMA
    piece = pltpu.VMEM((nch, rows, WIDE), F32)
    whole = pltpu.VMEM((nch, sites, WIDE), F32)
    done = pl.pallas_call(
        functools.partial(kernel, n_t, n_r),
        out_shape=jax.ShapeDtypeStruct((1, rows, sites), F32),
        in_specs=[
            pl.BlockSpec(memory_space=pltpu.HBM),
            pl.BlockSpec(memory_space=pltpu.HBM),
        ],
        out_specs=pl.BlockSpec(memory_space=pltpu.VMEM),
        scratch_shapes=[
            pltpu.VMEM((rows, sites), F32),
            pltpu.VMEM((1, rows), F32),
            whole,
            whole,
            piece,
            pltpu.VMEM((2 * rows, sites), BF16),
            pltpu.VMEM((2 * rows, sites), BF16),
            pltpu.VMEM((sites, sites), BF16),
            pltpu.VMEM((sites, sites), BF16),
            pltpu.VMEM((sites, sites), BF16),
            pltpu.VMEM((sites, sites), BF16),
            piece,
            piece,
            piece,
            piece,
            pltpu.VMEM((FOLD * WIDE, sites), BF16),
            pltpu.VMEM((FOLD * WIDE, sites), BF16),
            pltpu.VMEM((2, rows, WIDE), F32),
            dma((nch + 1,)),
            pltpu.SemaphoreType.REGULAR,
            dma((2,)),
            dma((2,)),
            dma((2, nch)),
            dma((2, nch)),
            dma((2, nch)),
            dma((2, nch)),
            dma((nch,)),
            dma((nch,)),
            dma((nch,)),
            dma((nch,)),
            dma((nch,)),
            dma((nch,)),
            dma((nch,)),
            dma((nch,)),
            dma((nch,)),
            dma((nch,)),
        ],
        compiler_params=pltpu.CompilerParams(
            collective_id=0, has_side_effects=True, vmem_limit_bytes=52 * 2**20
        ),
        cost_estimate=pl.CostEstimate(
            flops=18 * rows * sites * sites, bytes_accessed=8 * rows * sites, transcendentals=0
        ),
    )(coupling, field)
    pieces = 4

    def write(src, dst, sems):
        step = rows // pieces
        copies = [
            pltpu.make_async_copy(
                src.at[0, pl.ds(i * step, step)], dst.at[0, pl.ds(i * step, step)], sems.at[i]
            )
            for i in range(pieces)
        ]
        for c in copies:
            c.start()
        for c in copies:
            c.wait()

    return pl.pallas_call(
        write,
        out_shape=jax.ShapeDtypeStruct((1, rows, sites), F32),
        in_specs=[pl.BlockSpec(memory_space=pl.ANY)],
        out_specs=pl.BlockSpec(memory_space=pl.ANY),
        scratch_shapes=[dma((pieces,))],
        compiler_params=pltpu.CompilerParams(vmem_limit_bytes=2**20),
    )(done)


def solution(mesh):
    return jax.shard_map(
        functools.partial(per_device, mesh.shape["tm"], mesh.shape["rows"]),
        mesh=mesh,
        in_specs=(P("tm", "rows", None), P("tm", "rows")),
        out_specs=P("tm", "rows", None),
        check_vma=False,
    )
```

```python
import functools

import jax
import jax.numpy as jnp
from jax import lax
from jax.experimental import pallas as pl
from jax.experimental.pallas import tpu as pltpu
from jax.sharding import PartitionSpec as P

F32 = jnp.float32
BF16 = jnp.bfloat16
MESH = pl.DeviceIdType.MESH

WIDE = 128
AHEAD = 2
FOLD = 2
LEAD = 1
START = 5


def split(x):
    hi = x.astype(BF16)
    return hi, (x - hi.astype(F32)).astype(BF16)


def dot3(ah, al, bh, bl):
    def mm(a, b):
        return jnp.dot(a, b, preferred_element_type=F32)

    return mm(ah, bh) + (mm(ah, bl) + mm(al, bh))


def kernel(
    n_t, n_r, coupling, field, out,
    raw, levels, full, sib, rowbuf, lhs_h, lhs_l, own_h, own_l, one_h, one_l,
    stage_a, stage_b, land_a, land_b, meet_h, meet_l,
    rel, load_sem, pace, rel_s, rel_r,
    own_s, own_r, fwd_s, fwd_r, sib_s, sib_r, xo_s, xo_r, row_s, row_r, a_s, a_r, b_s, b_r,
):
    t = lax.axis_index("tm")
    r = lax.axis_index("rows")
    rows = coupling.shape[1]
    nch = full.shape[0]
    even = lax.rem(t, 2) == 0
    half = rows // 2
    span = n_t // 2
    place = lax.rem(t, span)
    base = t - place
    other = span - base
    line = 16
    n_rel = (nch, nch - 1, nch - 1)
    odd = jnp.logical_not(even)
    is_src = place == 0
    is_dst = place >= span - 2
    kind = place // line - 1
    mine = lax.rem(place, line) // 2
    is_rel = jnp.logical_or(
        jnp.logical_and(even, kind == 0),
        jnp.logical_and(odd, jnp.logical_and(kind > 0, mine < n_rel[1])),
    )

    def way(k, c):
        return (k + 1) * line + 2 * c + (1 if k else 0)

    def tm(by):
        return lax.rem(t + by + n_t, n_t)

    def at_t(by):
        return (tm(by), r)

    def at_r(by):
        return (t, lax.rem(r + by + n_r, n_r))

    def plane(by):
        return pl.multiple_of(lax.rem(r + by + n_r, n_r) * rows, rows)

    def cols(c):
        return pl.ds(pl.multiple_of(c * WIDE, WIDE), WIDE)

    def load(c):
        src = coupling.at[0, :, cols(c)]
        return pltpu.make_async_copy(src, raw.at[:, cols(c)], load_sem.at[c])

    load_levels = pltpu.make_async_copy(field, levels, load_sem.at[nch])
    load_levels.start()
    for c in range(nch):
        load(c).start()

    barrier = pltpu.get_barrier_semaphore()
    for by in (1, -1):
        pl.semaphore_signal(barrier, inc=1, device_id=at_r(by), device_id_type=MESH)
    pl.semaphore_signal(barrier, inc=1, device_id=at_t(1), device_id_type=MESH)

    @pl.when(even)
    def _():
        pl.semaphore_signal(barrier, inc=1, device_id=at_t(2), device_id_type=MESH)

    @pl.when(is_rel)
    def _():
        for to in (base, other + place):
            pl.semaphore_signal(barrier, inc=1, device_id=(to, r), device_id_type=MESH)

    beside = (other + place, r)
    pl.semaphore_signal(barrier, inc=1, device_id=beside, device_id_type=MESH)

    def greet(k):
        for c in range(n_rel[k]):
            to = (base + way(k, c), r)
            pl.semaphore_signal(barrier, inc=1, device_id=to, device_id_type=MESH)

    @pl.when(jnp.logical_and(is_dst, even))
    def _():
        greet(1)

    @pl.when(jnp.logical_and(is_dst, odd))
    def _():
        greet(0)
        greet(2)

    def copy(src, dst, ssem, rsem, dev):
        return pltpu.make_async_remote_copy(
            src_ref=src, dst_ref=dst, send_sem=ssem, recv_sem=rsem,
            device_id=dev, device_id_type=MESH,
        )

    def own(c, d):
        piece = full.at[c, pl.ds(plane(0), rows), :]
        return copy(piece, piece, own_s.at[d, c], own_r.at[d, c], at_r(1 - 2 * d))

    def own_in(c, d):
        piece = full.at[c, pl.ds(plane(2 * d - 1), rows), :]
        return copy(piece, piece, own_s.at[d, c], own_r.at[d, c], at_r(1 - 2 * d))

    def fwd(c, d):
        piece = full.at[c, pl.ds(pl.multiple_of(plane(2 * d - 1) + d * half, half), half), :]
        return copy(piece, piece, fwd_s.at[d, c], fwd_r.at[d, c], at_r(1 - 2 * d))

    def fwd_in(c, d):
        piece = full.at[c, pl.ds(pl.multiple_of(plane(2) + d * half, half), half), :]
        return copy(piece, piece, fwd_s.at[d, c], fwd_r.at[d, c], at_r(1 - 2 * d))

    def to_sib(c):
        return copy(full.at[c], sib.at[c], sib_s.at[c], sib_r.at[c], at_t(-1))

    def xo(c):
        return copy(stage_a.at[c], land_a.at[c], xo_s.at[c], xo_r.at[c], at_t(-1))

    def row(c):
        piece = full.at[c, pl.ds(plane(0), rows), :]
        return copy(piece, rowbuf.at[c], row_s.at[c], row_r.at[c], at_t(-1))

    def send_a(c):
        return copy(stage_a.at[c], land_b.at[c], a_s.at[c], a_r.at[c], at_t(-2))

    def send_b(c):
        return copy(stage_b.at[c], land_b.at[c], b_s.at[c], b_r.at[c], at_t(-1))

    def by_way(k, c):
        src = (full.at[c, pl.ds(plane(0), rows), :], stage_a.at[c], stage_b.at[c])[k]
        sem = (row_s, a_s, b_s)[k].at[c]
        return copy(src, rel.at[0], sem, rel_r.at[0], (base + way(k, c), r))

    def start(k, c):
        go = (row, send_a, send_b)[k]
        by = jnp.logical_and(is_src, c < n_rel[k])

        @pl.when(by)
        def _():
            by_way(k, c).start()

        @pl.when(jnp.logical_not(by))
        def _():
            go(c).start()

    def over():
        return copy(rel.at[0], rel.at[1], rel_s.at[0], rel_r.at[1], (other + place, r))

    def last_leg(k):
        dst, sem, back = ((rowbuf, row_r, 1), (land_b, a_r, 2), (land_b, b_r, 1))[k]
        to = (lax.rem(other - back + n_t, n_t), r)
        return copy(rel.at[1], dst.at[mine], rel_s.at[1], sem.at[mine], to)

    def hand_on(kinds):
        @pl.when(is_rel)
        def _():
            copy(rel.at[0], rel.at[0], rel_s.at[0], rel_r.at[0], (base, r)).wait_recv()
            over().start()
            over().wait_recv()

        for k in kinds:

            @pl.when(jnp.logical_and(is_rel, kind == k))
            def _():
                last_leg(k).start()

    def handed(kinds):
        for k in kinds:

            @pl.when(jnp.logical_and(is_rel, kind == k))
            def _():
                over().wait_send()
                last_leg(k).wait_send()

    load_levels.wait()
    scale = jnp.exp(jnp.transpose(jnp.broadcast_to(levels[...], (WIDE, rows))))
    row_ids = lax.broadcasted_iota(jnp.int32, (rows, WIDE), 0) + r * rows
    col_ids = lax.broadcasted_iota(jnp.int32, (rows, WIDE), 1)

    def build(c, _):
        load(c).wait()
        ident = jnp.where(row_ids == col_ids + c * WIDE, 1.0, 0.0).astype(F32)
        full[c, pl.ds(plane(0), rows), :] = scale * (ident + raw[:, cols(c)])
        return 0

    lax.fori_loop(0, AHEAD, build, 0)

    def rest_of_block():
        lax.fori_loop(AHEAD, nch, build, 0)

        def send(c, _):
            start(0, c)

            @pl.when(is_src)
            def _():
                row(c).wait_send()

            return 0

        lax.fori_loop(0, nch, send, 0)

    def gather(process, before):
        for c in range(AHEAD):
            for d in (0, 1):
                own(c, d).start()
        before()

        def step(c, _):
            @pl.when(c < nch)
            def _():
                for d in (0, 1):
                    own_in(c, d).wait_recv()
                    fwd(c, d).start()

            @pl.when(c + AHEAD + LEAD < nch)
            def _():
                pl.semaphore_signal(pace, inc=1, device_id=beside, device_id_type=MESH)

            @pl.when(c + AHEAD < nch)
            def _():
                @pl.when(c >= LEAD)
                def _():
                    pl.semaphore_wait(pace, 1)

                for d in (0, 1):
                    own(c + AHEAD, d).start()

            @pl.when(c >= 1)
            def _():
                for d in (0, 1):
                    fwd_in(c - 1, d).wait_recv()
                process(c - 1)

            return 0

        lax.fori_loop(0, nch + 1, step, 0)

    def drain(c, _):
        for d in (0, 1):
            own(c, d).wait_send()
            fwd(c, d).wait_send()
        return 0

    def fill_lhs(c, first):
        hi, lo = split(rowbuf[c])
        lhs_h[first : first + rows, cols(c)] = hi
        lhs_l[first : first + rows, cols(c)] = lo

    def add_chunk(c):
        h, l = split(land_b[c])
        out[0] += dot3(h, l, one_h[cols(c), :], one_l[cols(c), :])

    @pl.when(jnp.logical_not(even))
    def _():
        pl.semaphore_wait(barrier, jnp.where(is_rel, 6, 4))

        def left_factor():
            def body(c, _):
                row(c).wait_recv()
                fill_lhs(c, 0)
                return 0

            lax.fori_loop(0, nch, body, 0)

        def product(c, _):
            stage_a[c] = dot3(
                lhs_h[0:rows, :], lhs_l[0:rows, :], one_h[:, cols(c)], one_l[:, cols(c)]
            )
            xo(c).start()
            return 0

        lag = 5

        def process(c):
            to_sib(c).start()
            hi, lo = split(full[c])
            one_h[:, cols(c)] = hi
            one_l[:, cols(c)] = lo

            @pl.when(c == lag)
            def _():
                left_factor()
                lax.fori_loop(0, lag, product, 0)

            @pl.when(c >= lag)
            def _():
                product(c, 0)

        gather(process, rest_of_block)
        out[...] = jnp.zeros_like(out)

        def body(c, _):
            @pl.when(c == mine)
            def _():
                hand_on((1, 2))

            send_b(c).wait_recv()
            add_chunk(c)
            return 0

        lax.fori_loop(0, nch, body, 0)

        def finish(c, _):
            row(c).wait_send()
            to_sib(c).wait_send()
            xo(c).wait_send()
            return 0

        lax.fori_loop(0, nch, finish, 0)
        lax.fori_loop(0, nch, drain, 0)

        handed((1, 2))
    @pl.when(even)
    def _():
        pl.semaphore_wait(barrier, jnp.where(is_src, 5 + sum(n_rel), jnp.where(is_rel, 7, 5)))
        rest_of_block()

        hand_on((0,))

        def fill(c, _):
            row(c).wait_recv()
            fill_lhs(c, 0)
            return 0

        lax.fori_loop(0, nch, fill, 0)

        def take(c, _):
            to_sib(c).wait_recv()
            hi, lo = split(sib[c])
            one_h[:, cols(c)] = hi
            one_l[:, cols(c)] = lo
            return 0

        lax.fori_loop(0, START, take, 0)
        def process(c):
            @pl.when(c == 0)
            def _():
                lax.fori_loop(START, nch, take, 0)

                def body(k, _):
                    xo(k).wait_recv()
                    hi, lo = split(land_a[k])
                    lhs_h[rows : 2 * rows, cols(k)] = hi
                    lhs_l[rows : 2 * rows, cols(k)] = lo
                    return 0

                lax.fori_loop(0, nch, body, 0)

            bh, bl = split(full[c])
            own_h[:, cols(c)] = bh
            own_l[:, cols(c)] = bl
            stage_a[c] = dot3(lhs_h[0:rows, :], lhs_l[0:rows, :], bh, bl)
            start(1, c)
            stage_b[c] = dot3(lhs_h[rows:, :], lhs_l[rows:, :], bh, bl)
            start(2, c)

        gather(process, lambda: None)

        def collect(c, _):
            send_a(c).wait_recv()
            hi, lo = split(land_b[c])
            lhs_h[0:rows, cols(c)] = hi
            lhs_l[0:rows, cols(c)] = lo
            return 0

        lax.fori_loop(0, nch - FOLD, collect, 0)

        cut = (nch - FOLD) * WIDE
        wide = 2 * WIDE
        parts = [slice(k * wide, (k + 1) * wide) for k in range(nch // 2)]
        fh, fl = lhs_h[0:rows, 0:cut], lhs_l[0:rows, 0:cut]
        for part in parts:
            x = dot3(fh, fl, one_h[0:cut, part], one_l[0:cut, part])
            lhs_h[rows:, part], lhs_l[rows:, part] = split(x)
        xh, xl = lhs_h[rows:, :], lhs_l[rows:, :]
        gh, gl = one_h[cut:, :], one_l[cut:, :]
        for part in parts:
            vh, vl = own_h[:, part], own_l[:, part]
            out[0, :, part] = dot3(xh, xl, vh, vl)
            meet_h[:, part], meet_l[:, part] = split(dot3(gh, gl, vh, vl))

        lax.fori_loop(nch - FOLD, nch, collect, 0)
        lh, ll = lhs_h[0:rows, cut:], lhs_l[0:rows, cut:]
        for part in parts:
            out[0, :, part] += dot3(lh, ll, meet_h[:, part], meet_l[:, part])

        def finish(c, _):
            @pl.when(jnp.logical_not(is_src))
            def _():
                row(c).wait_send()

            send_a(c).wait_send()
            send_b(c).wait_send()
            return 0

        lax.fori_loop(0, nch, finish, 0)
        lax.fori_loop(0, nch, drain, 0)

        handed((0,))


def per_device(n_t, n_r, coupling, field):
    _, rows, sites = coupling.shape
    nch = sites // WIDE
    dma = pltpu.SemaphoreType.DMA
    piece = pltpu.VMEM((nch, rows, WIDE), F32)
    whole = pltpu.VMEM((nch, sites, WIDE), F32)
    done = pl.pallas_call(
        functools.partial(kernel, n_t, n_r),
        out_shape=jax.ShapeDtypeStruct((1, rows, sites), F32),
        in_specs=[
            pl.BlockSpec(memory_space=pltpu.HBM),
            pl.BlockSpec(memory_space=pltpu.HBM),
        ],
        out_specs=pl.BlockSpec(memory_space=pltpu.VMEM),
        scratch_shapes=[
            pltpu.VMEM((rows, sites), F32),
            pltpu.VMEM((1, rows), F32),
            whole,
            whole,
            piece,
            pltpu.VMEM((2 * rows, sites), BF16),
            pltpu.VMEM((2 * rows, sites), BF16),
            pltpu.VMEM((sites, sites), BF16),
            pltpu.VMEM((sites, sites), BF16),
            pltpu.VMEM((sites, sites), BF16),
            pltpu.VMEM((sites, sites), BF16),
            piece,
            piece,
            piece,
            piece,
            pltpu.VMEM((FOLD * WIDE, sites), BF16),
            pltpu.VMEM((FOLD * WIDE, sites), BF16),
            pltpu.VMEM((2, rows, WIDE), F32),
            dma((nch + 1,)),
            pltpu.SemaphoreType.REGULAR,
            dma((2,)),
            dma((2,)),
            dma((2, nch)),
            dma((2, nch)),
            dma((2, nch)),
            dma((2, nch)),
            dma((nch,)),
            dma((nch,)),
            dma((nch,)),
            dma((nch,)),
            dma((nch,)),
            dma((nch,)),
            dma((nch,)),
            dma((nch,)),
            dma((nch,)),
            dma((nch,)),
        ],
        compiler_params=pltpu.CompilerParams(
            collective_id=0, has_side_effects=True, vmem_limit_bytes=52 * 2**20
        ),
        cost_estimate=pl.CostEstimate(
            flops=18 * rows * sites * sites, bytes_accessed=8 * rows * sites, transcendentals=0
        ),
    )(coupling, field)
    pieces = 8

    def write(src, dst, sems):
        step = rows // pieces
        copies = [
            pltpu.make_async_copy(
                src.at[0, pl.ds(i * step, step)], dst.at[0, pl.ds(i * step, step)], sems.at[i]
            )
            for i in range(pieces)
        ]
        for c in copies:
            c.start()
        for c in copies:
            c.wait()

    return pl.pallas_call(
        write,
        out_shape=jax.ShapeDtypeStruct((1, rows, sites), F32),
        in_specs=[pl.BlockSpec(memory_space=pl.ANY)],
        out_specs=pl.BlockSpec(memory_space=pl.ANY),
        scratch_shapes=[dma((pieces,))],
        compiler_params=pltpu.CompilerParams(vmem_limit_bytes=2**20),
    )(done)


def solution(mesh):
    return jax.shard_map(
        functools.partial(per_device, mesh.shape["tm"], mesh.shape["rows"]),
        mesh=mesh,
        in_specs=(P("tm", "rows", None), P("tm", "rows")),
        out_specs=P("tm", "rows", None),
        check_vma=False,
    )
```
